256 devices in a mesh: dp: 32 (over y, z), seq: 8 (over x, core).
Axes of the slice: x: 4, y: 4, z: 8, core: 2. Of those that a mesh axis runs over, the one named last changes fastest.
Arguments:
- queries: bfloat16 [32, 1024, 2048], P('dp', 'seq'), may hold values from -6 to 6
- keys: bfloat16 [32, 1024, 2048], P('dp', 'seq'), may hold values from -6 to 6
- values: bfloat16 [32, 1024, 2048], P('dp', 'seq'), may hold values from -6 to 6
- grad_out: bfloat16 [32, 1024, 2048], P('dp', 'seq'), may hold values from -6 to 6
- q_gain: float32 [128], replicated, may hold values from 0.5 to 2
- k_gain: float32 [128], replicated, may hold values from 0.5 to 2
- clip_blocks: int32 [32], replicated, may hold values from 1 to 8, as said below
Outputs:
- attended: bfloat16 [32, 1024, 2048], P('dp', 'seq')
- grad_queries: bfloat16 [32, 1024, 2048], P('dp', 'seq')
- grad_keys: bfloat16 [32, 1024, 2048], P('dp', 'seq')
- grad_values: bfloat16 [32, 1024, 2048], P('dp', 'seq')
- grad_q_gain: float32 [128], replicated
- grad_k_gain: float32 [128], replicated
The draws below stay inside these ranges and needn't reach their ends.
Inputs may be any that keep to these rules, and one draw needn't show every extreme that they name: `clip_blocks`: one clip has exactly 8 blocks; the others have at most 4.
All inputs are finite; a program needn't handle non-finite values.
Results may differ from the reference program's by a relative error of at most 0.011.
Values may be sent and summed in bfloat16 or wider, within the bound.
A program may use at most 64 MiB of HBM per device.

```python
import math
import jax
import jax.numpy as jnp
from jax import lax

H = 16
DH = 128
BLOCK = 128
L = 1024
CLIPS = 32
BLOCKS_CLIP = 8


def draw_clip_blocks(key, part):
    key = jax.random.fold_in(key, 7)
    first_key, second_key = jax.random.split(key)
    shorter = max(BLOCKS_CLIP // 2, 1)
    lengths = jax.random.randint(first_key, (CLIPS,), 1, shorter + 1)
    longest = jax.random.randint(second_key, (), 0, CLIPS)
    return jnp.where(jnp.arange(CLIPS) == longest, BLOCKS_CLIP, lengths).astype(jnp.int32)


def block_scale(rng, extent, cuts, least, top_value):
    loudness, own = 1.0, jax.random.fold_in(rng, 6)
    for axis_at, parts in cuts:
        steps = jnp.exp(jax.random.uniform(jax.random.fold_in(own, axis_at), (parts,), jnp.float32, least / len(cuts), top_value / len(cuts)))
        loudness = loudness * jnp.repeat(steps, extent[axis_at] // parts).reshape([-1 if axis == axis_at else 1 for axis in range(len(extent))])
    return loudness


def noise(rng, extent, width, most, cuts=(), dtype=jnp.bfloat16):
    level = block_scale(rng, extent, cuts, -0.22, 0.18) if cuts else 1.0
    entries = jax.random.normal(rng, extent, jnp.float32) * width * level
    return jnp.minimum(jnp.maximum(entries, -most), most).astype(dtype)


def setup_inputs(seed: int = 0) -> dict:
    key_of = jax.random.split(jax.random.key(seed), 8)
    queries = noise(key_of[0], (CLIPS, L, H * DH), 1.0, 6.0, ((0, 32), (1, 8)))
    keys = noise(key_of[1], (CLIPS, L, H * DH), 1.0, 6.0, ((0, 32), (1, 8)))
    values = noise(key_of[2], (CLIPS, L, H * DH), 1.0, 6.0, ((0, 32), (1, 8)))
    grad_out = noise(key_of[3], (CLIPS, L, H * DH), 1.0, 6.0, ((0, 32), (1, 8)))
    q_gain = jnp.clip(jnp.exp(jax.random.uniform(key_of[4], (DH,), jnp.float32, math.log(0.5), math.log(2.0))), 0.5, 2.0)
    k_gain = jnp.clip(jnp.exp(jax.random.uniform(key_of[5], (DH,), jnp.float32, math.log(0.5), math.log(2.0))), 0.5, 2.0)
    clip_blocks = draw_clip_blocks(jax.random.fold_in(key_of[7], 71), 0)
    return dict(queries=queries, keys=keys, values=values, grad_out=grad_out, q_gain=q_gain, k_gain=k_gain, clip_blocks=clip_blocks)


NORM_EPSILON = 1e-06

def normalize(inputs, gain_vec):
    inverse_rms = lax.rsqrt(lax.optimization_barrier(jnp.mean(inputs * inputs, axis=-1, keepdims=True)) + NORM_EPSILON)
    return (inputs * inverse_rms * gain_vec, inverse_rms)

def norm_back(inputs, inverse_rms, gain_vec, upstream):
    scaled = upstream * gain_vec
    cubed = inverse_rms * inverse_rms * inverse_rms
    grad_in = inverse_rms * scaled - inputs * cubed * lax.optimization_barrier(jnp.mean(scaled * inputs, axis=-1, keepdims=True))
    grad_gain = lax.optimization_barrier(jnp.sum(upstream * inputs * inverse_rms, axis=0))
    return (grad_in, grad_gain)

def head_full(q_rows, k_rows, v_rows, g_rows, length, q_gain, k_gain):
    softmax_scale = 1.0 / math.sqrt(q_rows.shape[-1])
    q_float = q_rows.astype(jnp.float32)
    k_float = k_rows.astype(jnp.float32)
    q_normed, q_rms = normalize(q_float, q_gain)
    k_normed, k_rms = normalize(k_float, k_gain)
    q_half = q_normed.astype(jnp.bfloat16)
    k_half = k_normed.astype(jnp.bfloat16)
    live_rows = jnp.arange(q_rows.shape[0]) < length
    scores = jnp.dot(q_half, k_half.T, preferred_element_type=jnp.float32) * softmax_scale
    scores = jnp.where(live_rows[None, :], scores, -1e+30)
    probs = jnp.exp(scores - lax.optimization_barrier(jnp.max(scores, axis=-1, keepdims=True)))
    probs = probs / lax.optimization_barrier(jnp.sum(probs, axis=-1, keepdims=True))
    probs = jnp.where(live_rows[:, None], probs, 0.0)
    probs_half = probs.astype(jnp.bfloat16)
    out_full = jnp.dot(probs_half, v_rows, preferred_element_type=jnp.float32)
    grad_v = jnp.dot(probs_half.T, g_rows, preferred_element_type=jnp.float32)
    grad_probs = jnp.dot(g_rows, v_rows.T, preferred_element_type=jnp.float32)
    row_dot = lax.optimization_barrier(jnp.sum(g_rows.astype(jnp.float32) * out_full, axis=-1, keepdims=True))
    grad_scores = (probs * (grad_probs - row_dot) * softmax_scale).astype(jnp.bfloat16)
    grad_qnorm = jnp.dot(grad_scores, k_half, preferred_element_type=jnp.float32)
    grad_knorm = jnp.dot(grad_scores.T, q_half, preferred_element_type=jnp.float32)
    grad_q, gain_q = norm_back(q_float, q_rms, q_gain, grad_qnorm)
    grad_k, gain_k = norm_back(k_float, k_rms, k_gain, grad_knorm)
    return (out_full.astype(jnp.bfloat16), grad_q.astype(jnp.bfloat16), grad_k.astype(jnp.bfloat16), grad_v.astype(jnp.bfloat16), gain_q, gain_k)

def reference(queries, keys, values, grad_out, q_gain, k_gain, clip_blocks):
    head_width = q_gain.shape[0]

    def split_heads(matrix):
        return matrix.reshape(matrix.shape[0], -1, head_width).transpose(1, 0, 2)

    def join_heads(stacked):
        return stacked.transpose(1, 0, 2).reshape(stacked.shape[1], -1)

    def one_clip(clip_items):
        q_clip, k_clip, v_clip, g_clip, blocks = clip_items
        length = blocks * BLOCK
        outcome = lax.map(lambda head_items: head_full(head_items[0], head_items[1], head_items[2], head_items[3], length, q_gain, k_gain), (split_heads(q_clip), split_heads(k_clip), split_heads(v_clip), split_heads(g_clip)))
        return (join_heads(outcome[0]), join_heads(outcome[1]), join_heads(outcome[2]), join_heads(outcome[3]), lax.optimization_barrier(jnp.sum(outcome[4], axis=0)), lax.optimization_barrier(jnp.sum(outcome[5], axis=0)))
    result = lax.map(one_clip, (queries, keys, values, grad_out, clip_blocks))
    return (result[0], result[1], result[2], result[3], lax.optimization_barrier(jnp.sum(result[4], axis=0)), lax.optimization_barrier(jnp.sum(result[5], axis=0)))
```

```python
import functools
import math

import jax
import jax.numpy as jnp
from jax import lax
from jax.experimental import pallas as pl
from jax.experimental.pallas import tpu as pltpu
from jax.sharding import PartitionSpec as P

BLOCK = 128
NORM_EPSILON = 1e-06
MESH = pl.DeviceIdType.MESH
QROWS = 256
NT = (((1,), (1,)), ((), ()))
NN = (((1,), (0,)), ((), ()))


def dot(a, b, dims):
    return lax.dot_general(a, b, dims, preferred_element_type=jnp.float32)


def inverse_rms(x):
    return lax.rsqrt(jnp.mean(x * x, axis=-1, keepdims=True) + NORM_EPSILON)


def norm_back(x, r, gain, upstream):
    scaled = upstream * gain
    mean = jnp.mean(scaled * x, axis=-1, keepdims=True)
    grad = r * scaled - x * (r * r * r * mean)
    return grad, jnp.sum(upstream * x * r, axis=0, keepdims=True)


def kernel(sizes, heads, q_ref, k_ref, v_ref, g_ref, qg_ref, kg_ref, blocks_ref,
           o_ref, dq_ref, dk_ref, dv_ref, gain_ref,
           inb, outb, keyc, keyt, valm, valt, dk_acc, dv_acc, red_a, red_b, red_c,
           in_send, in_recv, out_send, out_recv, red_send, red_recv):
    n, ny, nz = sizes
    dp = lax.axis_index("dp")
    me = lax.axis_index("seq")
    y, z = dp // nz, lax.rem(dp, nz)
    ins = (q_ref, k_ref, g_ref, v_ref)
    outs = (o_ref, dq_ref, dk_ref, dv_ref)
    rows = q_ref.shape[1]
    total = rows * n
    width = qg_ref.shape[1]

    barrier = pltpu.get_barrier_semaphore()
    for d in range(1, n):
        pl.semaphore_signal(barrier, inc=1, device_id=(dp, lax.rem(me + d, n)), device_id_type=MESH)
    for d in range(1, ny):
        pl.semaphore_signal(barrier, inc=1, device_id=(lax.rem(y + d, ny) * nz + z, me), device_id_type=MESH)
    for d in range(1, nz):
        pl.semaphore_signal(barrier, inc=1, device_id=(y * nz + lax.rem(z + d, nz), me), device_id_type=MESH)
    pl.semaphore_wait(barrier, n + ny + nz - 3)

    my_rows = pl.ds(pl.multiple_of(me * rows, rows), rows)

    def head_columns(device, j):
        return pl.ds(pl.multiple_of((device * heads + j) * width, width), width)

    for j in range(heads):
        for a in range(4):
            pltpu.make_async_copy(
                ins[a].at[0, :, head_columns(me, j)], inb.at[a, j, my_rows, :], in_recv.at[j, a]
            ).start()

        def send(d, carry, j=j):
            peer = lax.rem(me + d, n)
            for a in range(4):
                pltpu.make_async_remote_copy(
                    src_ref=ins[a].at[0, :, head_columns(peer, j)],
                    dst_ref=inb.at[a, j, my_rows, :],
                    send_sem=in_send.at[j, a],
                    recv_sem=in_recv.at[j, a],
                    device_id=(dp, peer),
                    device_id_type=MESH,
                ).start()
            return carry

        lax.fori_loop(1, n, send, 0)

    length = blocks_ref[dp] * BLOCK
    q_gain = qg_ref[...]
    k_gain = kg_ref[...]
    scale = 1.0 / math.sqrt(width)
    key_scale = scale * math.log2(math.e)
    live_col = lax.broadcasted_iota(jnp.int32, (total, 1), 0) < length
    gain_q = jnp.zeros((1, width), jnp.float32)
    gain_k = jnp.zeros((1, width), jnp.float32)

    for j in range(heads):
        for a in range(4):
            pltpu.make_async_copy(inb.at[a, j], inb.at[a, j], in_recv.at[j, a]).wait()
        k_float = inb[1, j].astype(jnp.float32)
        k_normed = jnp.where(live_col, k_float * inverse_rms(k_float) * (k_gain * key_scale), 0.0)
        keyc[...] = k_normed.astype(jnp.bfloat16)
        keyt[...] = k_normed.T.astype(jnp.bfloat16)
        v_float = jnp.where(live_col, inb[3, j].astype(jnp.float32), 0.0)
        valm[...] = v_float.astype(jnp.bfloat16)
        valt[0:width, :] = v_float.T.astype(jnp.bfloat16)
        live_lane = lax.broadcasted_iota(jnp.int32, (16, total), 1) < length
        valt[width:, :] = jnp.where(live_lane, 1.0, 0.0).astype(jnp.bfloat16)
        dk_acc[...] = jnp.zeros_like(dk_acc)
        dv_acc[...] = jnp.zeros_like(dv_acc)

        def block(i, gain_q, j=j):
            at = pl.ds(pl.multiple_of(i * QROWS, QROWS), QROWS)
            q_float = inb[0, j, at, :].astype(jnp.float32)
            r_q = inverse_rms(q_float)
            q_half = (q_float * r_q * q_gain).astype(jnp.bfloat16)
            e = jnp.exp2(dot(keyc[...], q_half, NT))
            e_half = e.astype(jnp.bfloat16)
            out_ext = dot(valt[...], e_half, NN)
            live = i * QROWS + lax.broadcasted_iota(jnp.int32, (1, QROWS), 1) < length
            inv = jnp.where(live, 1.0 / out_ext[width:width + 1, :], 0.0)
            out_t = out_ext[0:width, :] * inv
            g_t = inb[2, j, at, :].astype(jnp.float32).T * inv
            gs = g_t.astype(jnp.bfloat16)
            row_dot = jnp.sum(g_t * out_t, axis=0, keepdims=True)
            grad_probs = dot(valm[...], gs, NN)
            ds = (e * (grad_probs - row_dot)).astype(jnp.bfloat16)
            dv_acc[...] += dot(e_half, gs, NT)
            dk_acc[...] += dot(ds, q_half, NN)
            grad_qnorm = dot(keyt[...], ds, NN).T * math.log(2.0)
            grad_q, part = norm_back(q_float, r_q, q_gain, grad_qnorm)
            outb[0, j, at, :] = out_t.T.astype(jnp.bfloat16)
            outb[1, j, at, :] = grad_q.astype(jnp.bfloat16)
            return gain_q + part

        gain_q = lax.fori_loop(0, total // QROWS, block, gain_q)
        k_float = inb[1, j].astype(jnp.float32)
        grad_knorm = jnp.where(live_col, dk_acc[...] * scale, 0.0)
        grad_k, part = norm_back(k_float, inverse_rms(k_float), k_gain, grad_knorm)
        gain_k = gain_k + part
        outb[2, j] = grad_k.astype(jnp.bfloat16)
        outb[3, j] = jnp.where(live_col, dv_acc[...], 0.0).astype(jnp.bfloat16)

        for a in range(4):
            pltpu.make_async_copy(
                outb.at[a, j, my_rows, :], outs[a].at[0, :, head_columns(me, j)], out_recv.at[a]
            ).start()

        def give(d, carry, j=j):
            peer = lax.rem(me + d, n)
            for a in range(4):
                pltpu.make_async_remote_copy(
                    src_ref=outb.at[a, j, pl.ds(pl.multiple_of(peer * rows, rows), rows), :],
                    dst_ref=outs[a].at[0, :, head_columns(me, j)],
                    send_sem=out_send.at[j, a],
                    recv_sem=out_recv.at[a],
                    device_id=(dp, peer),
                    device_id_type=MESH,
                ).start()
            return carry

        lax.fori_loop(1, n, give, 0)

    part = jnp.concatenate([gain_q, gain_k, jnp.zeros((6, width), jnp.float32)], axis=0)
    stages = (
        (red_a, n, me, lambda p: (dp, p)),
        (red_b, ny, y, lambda p: (p * nz + z, me)),
        (red_c, nz, z, lambda p: (y * nz + p, me)),
    )
    for s, (slots, count, mine, place) in enumerate(stages):
        slots[mine] = part
        copies = []
        for d in range(1, count):
            copies.append(pltpu.make_async_remote_copy(
                src_ref=slots.at[mine],
                dst_ref=slots.at[mine],
                send_sem=red_send.at[s, d],
                recv_sem=red_recv.at[s, d],
                device_id=place(lax.rem(mine + d, count)),
                device_id_type=MESH,
            ))
        for copy in copies:
            copy.start()
        for copy in copies:
            copy.wait()
        part = slots[0]
        for p in range(1, count):
            part = part + slots[p]
    gain_ref[...] = part

    for j in range(heads):
        for a in range(4):
            pltpu.make_async_copy(
                inb.at[a, j, pl.ds(0, total - rows), :], inb.at[a, j, pl.ds(0, total - rows), :], in_send.at[j, a]
            ).wait()
            pltpu.make_async_copy(
                outb.at[a, j, pl.ds(0, total - rows), :], outb.at[a, j, pl.ds(0, total - rows), :], out_send.at[j, a]
            ).wait()
    for a in range(4):
        pltpu.make_async_copy(outs[a], outs[a], out_recv.at[a]).wait()


def shards(sizes, queries, keys, values, grad_out, q_gain, k_gain, clip_blocks):
    n, ny, nz = sizes
    rows, columns = queries.shape[1:]
    width = q_gain.shape[0]
    heads = columns // width // n
    total = rows * n
    hbm = pl.BlockSpec(memory_space=pl.ANY)
    vmem = pl.BlockSpec(memory_space=pltpu.VMEM)
    wide = jax.ShapeDtypeStruct(queries.shape, jnp.bfloat16)
    half, full = jnp.bfloat16, jnp.float32
    result = pl.pallas_call(
        functools.partial(kernel, sizes, heads),
        name="attention_exchange",
        out_shape=(wide, wide, wide, wide, jax.ShapeDtypeStruct((8, width), full)),
        in_specs=[hbm, hbm, hbm, hbm, vmem, vmem, pl.BlockSpec(memory_space=pltpu.SMEM)],
        out_specs=(hbm, hbm, hbm, hbm, vmem),
        scratch_shapes=[
            pltpu.VMEM((4, heads, total, width), half),
            pltpu.VMEM((4, heads, total, width), half),
            pltpu.VMEM((total, width), half),
            pltpu.VMEM((width, total), half),
            pltpu.VMEM((total, width), half),
            pltpu.VMEM((width + 16, total), half),
            pltpu.VMEM((total, width), full),
            pltpu.VMEM((total, width), full),
            pltpu.VMEM((n, 8, width), full),
            pltpu.VMEM((ny, 8, width), full),
            pltpu.VMEM((nz, 8, width), full),
            pltpu.SemaphoreType.DMA((heads, 4)),
            pltpu.SemaphoreType.DMA((heads, 4)),
            pltpu.SemaphoreType.DMA((heads, 4)),
            pltpu.SemaphoreType.DMA((4,)),
            pltpu.SemaphoreType.DMA((3, 8)),
            pltpu.SemaphoreType.DMA((3, 8)),
        ],
        compiler_params=pltpu.CompilerParams(
            collective_id=0, has_side_effects=True, vmem_limit_bytes=48 * 2**20
        ),
    )(queries, keys, values, grad_out, q_gain.reshape(1, width), k_gain.reshape(1, width), clip_blocks)
    attended, grad_q, grad_k, grad_v, gains = result
    return attended, grad_q, grad_k, grad_v, gains[0], gains[1]


def solution(mesh):
    n = mesh.shape["seq"]
    nz = 8
    ny = mesh.shape["dp"] // nz
    placed = P("dp", "seq", None)
    return jax.shard_map(
        functools.partial(shards, (n, ny, nz)),
        mesh=mesh,
        in_specs=(placed, placed, placed, placed, P(), P(), P()),
        out_specs=(placed, placed, placed, placed, P(), P()),
        check_vma=False,
    )
```

```python
import functools
import math

import jax
import jax.numpy as jnp
from jax import lax
from jax.experimental import pallas as pl
from jax.experimental.pallas import tpu as pltpu
from jax.sharding import PartitionSpec as P

BLOCK = 128
NORM_EPSILON = 1e-06
MESH = pl.DeviceIdType.MESH
QROWS = 256
HUB = 0
NT = (((1,), (1,)), ((), ()))
NN = (((1,), (0,)), ((), ()))


def dot(a, b, dims):
    return lax.dot_general(a, b, dims, preferred_element_type=jnp.float32)


def inverse_rms(x):
    return lax.rsqrt(jnp.mean(x * x, axis=-1, keepdims=True) + NORM_EPSILON)


def norm_back(x, r, gain, upstream):
    scaled = upstream * gain
    mean = jnp.mean(scaled * x, axis=-1, keepdims=True)
    grad = r * scaled - x * (r * r * r * mean)
    return grad, jnp.sum(upstream * x * r, axis=0, keepdims=True)


def kernel(sizes, heads, q_ref, k_ref, v_ref, g_ref, qg_hbm, kg_hbm, blocks_hbm,
           o_ref, dq_ref, dk_ref, dv_ref, gain_ref,
           qg_ref, kg_ref, blocks_ref, small_sem, inb, outb, keyc, keyt, valm, valt, dk_acc, dv_acc, red_a, red_b, red_c, red_d, go_sem,
           in_send, in_recv, out_send, out_recv, red_send, red_recv):
    n, ny, nz = sizes
    dp = lax.axis_index("dp")
    me = lax.axis_index("seq")
    y, z = dp // nz, lax.rem(dp, nz)
    ins = (q_ref, k_ref, g_ref, v_ref)
    outs = (o_ref, dq_ref, dk_ref, dv_ref)
    rows = q_ref.shape[1]
    total = rows * n
    width = qg_ref.shape[1]

    smalls = [
        pltpu.make_async_copy(source, target, small_sem.at[i])
        for i, (source, target) in enumerate(
            ((qg_hbm, qg_ref), (kg_hbm, kg_ref), (blocks_hbm, blocks_ref))
        )
    ]
    for copy in smalls:
        copy.start()

    my_rows = pl.ds(pl.multiple_of(me * rows, rows), rows)

    def head_columns(device, j):
        return pl.ds(pl.multiple_of((device * heads + j) * width, width), width)

    for j in range(heads):
        for a in range(4):
            pltpu.make_async_copy(
                ins[a].at[0, :, head_columns(me, j)], inb.at[a, j, my_rows, :], in_recv.at[j, a]
            ).start()

    barrier = pltpu.get_barrier_semaphore()

    def greet(d, carry):
        peer = lax.rem(me + d, n)

        @pl.when(peer != HUB)
        def _():
            pl.semaphore_signal(barrier, inc=1, device_id=(dp, peer), device_id_type=MESH)

        return carry

    lax.fori_loop(1, n, greet, 0)

    @pl.when(me == HUB)
    def _():
        for d in range(1, ny):
            pl.semaphore_signal(barrier, inc=1, device_id=(lax.rem(y + d, ny) * nz + z, me), device_id_type=MESH)
        for d in range(1, nz):
            pl.semaphore_signal(barrier, inc=1, device_id=(y * nz + lax.rem(z + d, nz), me), device_id_type=MESH)

    @pl.when(me != HUB)
    def _():
        pl.semaphore_wait(barrier, n - 1)
        pl.semaphore_signal(go_sem, inc=1, device_id=(dp, HUB), device_id_type=MESH)

    @pl.when(me == HUB)
    def _():
        pl.semaphore_wait(go_sem, n - 1)

    for j in range(heads):
        def send(d, carry, j=j):
            peer = lax.rem(me + d, n)
            for a in range(4):
                pltpu.make_async_remote_copy(
                    src_ref=ins[a].at[0, :, head_columns(peer, j)],
                    dst_ref=inb.at[a, j, my_rows, :],
                    send_sem=in_send.at[j, a],
                    recv_sem=in_recv.at[j, a],
                    device_id=(dp, peer),
                    device_id_type=MESH,
                ).start()
            return carry

        lax.fori_loop(1, n, send, 0)

    for copy in smalls:
        copy.wait()
    length = blocks_ref[dp] * BLOCK
    q_gain = qg_ref[...]
    k_gain = kg_ref[...]
    scale = 1.0 / math.sqrt(width)
    key_scale = scale * math.log2(math.e)
    live_col = lax.broadcasted_iota(jnp.int32, (total, 1), 0) < length
    gain_q = jnp.zeros((1, width), jnp.float32)
    gain_k = jnp.zeros((1, width), jnp.float32)

    for j in range(heads):
        for a in range(4):
            pltpu.make_async_copy(inb.at[a, j], inb.at[a, j], in_recv.at[j, a]).wait()
        k_float = inb[1, j].astype(jnp.float32)
        k_normed = jnp.where(live_col, k_float * inverse_rms(k_float) * (k_gain * key_scale), 0.0)
        keyc[...] = k_normed.astype(jnp.bfloat16)
        keyt[...] = k_normed.T.astype(jnp.bfloat16)
        v_float = jnp.where(live_col, inb[3, j].astype(jnp.float32), 0.0)
        valm[...] = v_float.astype(jnp.bfloat16)
        valt[0:width, :] = v_float.T.astype(jnp.bfloat16)
        live_lane = lax.broadcasted_iota(jnp.int32, (16, total), 1) < length
        valt[width:, :] = jnp.where(live_lane, 1.0, 0.0).astype(jnp.bfloat16)
        dk_acc[...] = jnp.zeros_like(dk_acc)
        dv_acc[...] = jnp.zeros_like(dv_acc)

        def block(i, gain_q, j=j):
            at = pl.ds(pl.multiple_of(i * QROWS, QROWS), QROWS)
            q_float = inb[0, j, at, :].astype(jnp.float32)
            r_q = inverse_rms(q_float)
            q_half = (q_float * r_q * q_gain).astype(jnp.bfloat16)
            e = jnp.exp2(dot(keyc[...], q_half, NT))
            e_half = e.astype(jnp.bfloat16)
            out_ext = dot(valt[...], e_half, NN)
            live = i * QROWS + lax.broadcasted_iota(jnp.int32, (1, QROWS), 1) < length
            inv = jnp.where(live, 1.0 / out_ext[width:width + 1, :], 0.0)
            out_t = out_ext[0:width, :] * inv
            g_t = inb[2, j, at, :].astype(jnp.float32).T * inv
            gs = g_t.astype(jnp.bfloat16)
            row_dot = jnp.sum(g_t * out_t, axis=0, keepdims=True)
            grad_probs = dot(valm[...], gs, NN)
            ds = (e * (grad_probs - row_dot)).astype(jnp.bfloat16)
            dv_acc[...] += dot(e_half, gs, NT)
            dk_acc[...] += dot(ds, q_half, NN)
            grad_qnorm = dot(keyt[...], ds, NN).T * math.log(2.0)
            grad_q, part = norm_back(q_float, r_q, q_gain, grad_qnorm)
            outb[0, j, at, :] = out_t.T.astype(jnp.bfloat16)
            outb[1, j, at, :] = grad_q.astype(jnp.bfloat16)
            return gain_q + part

        gain_q = lax.fori_loop(0, total // QROWS, block, gain_q)
        k_float = inb[1, j].astype(jnp.float32)
        grad_knorm = jnp.where(live_col, dk_acc[...] * scale, 0.0)
        grad_k, part = norm_back(k_float, inverse_rms(k_float), k_gain, grad_knorm)
        gain_k = gain_k + part
        outb[2, j] = grad_k.astype(jnp.bfloat16)
        outb[3, j] = jnp.where(live_col, dv_acc[...], 0.0).astype(jnp.bfloat16)

        for a in range(4):
            pltpu.make_async_copy(
                outb.at[a, j, my_rows, :], outs[a].at[0, :, head_columns(me, j)], out_recv.at[a]
            ).start()

        def give_back(arrays, j=j):
            def give(d, carry):
                peer = lax.rem(me + d, n)
                for a in arrays:
                    pltpu.make_async_remote_copy(
                        src_ref=outb.at[a, j, pl.ds(pl.multiple_of(peer * rows, rows), rows), :],
                        dst_ref=outs[a].at[0, :, head_columns(me, j)],
                        send_sem=out_send.at[j, a],
                        recv_sem=out_recv.at[a],
                        device_id=(dp, peer),
                        device_id_type=MESH,
                    ).start()
                return carry

            lax.fori_loop(1, n, give, 0)

        if j < heads - 1:
            give_back(range(4))

    def small(source, target, stage, slot, device):
        return pltpu.make_async_remote_copy(
            src_ref=source, dst_ref=target, send_sem=red_send.at[stage, slot], recv_sem=red_recv.at[stage, slot],
            device_id=device, device_id_type=MESH,
        )

    def gathered(slots):
        part = slots[0]
        for p in range(1, slots.shape[0]):
            part = part + slots[p]
        return part

    red_a[me] = jnp.concatenate([gain_q, gain_k, jnp.zeros((6, width), jnp.float32)], axis=0)

    @pl.when(me != HUB)
    def _():
        up = small(red_a.at[me], red_a.at[me], 0, me, (dp, HUB))
        up.start()
        give_back(range(4))
        up.wait_send()
        small(red_d, red_d, 3, me, (dp, HUB)).wait_recv()

    @pl.when(me == HUB)
    def _():
        give_back((0,))
        for p in range(n):
            if p != HUB:
                small(red_a.at[p], red_a.at[p], 0, p, (dp, p)).wait_recv()
        red_b[y] = gathered(red_a)
        pl.semaphore_wait(barrier, ny + nz - 2)
        along_y = [
            small(red_b.at[y], red_b.at[y], 1, d, (lax.rem(y + d, ny) * nz + z, me)) for d in range(1, ny)
        ]
        for copy in along_y:
            copy.start()
        give_back((1,))
        for copy in along_y:
            copy.wait()
        red_c[z] = gathered(red_b)
        along_z = [
            small(red_c.at[z], red_c.at[z], 2, d, (y * nz + lax.rem(z + d, nz), me)) for d in range(1, nz)
        ]
        for copy in along_z:
            copy.start()
        give_back((2, 3))
        for copy in along_z:
            copy.wait()
        red_d[...] = gathered(red_c)
        down = [small(red_d, red_d, 3, p, (dp, p)) for p in range(n) if p != HUB]
        for copy in down:
            copy.start()
        for copy in down:
            copy.wait_send()

    gain_ref[...] = red_d[...]

    for j in range(heads):
        for a in range(4):
            pltpu.make_async_copy(
                inb.at[a, j, pl.ds(0, total - rows), :], inb.at[a, j, pl.ds(0, total - rows), :], in_send.at[j, a]
            ).wait()
            pltpu.make_async_copy(
                outb.at[a, j, pl.ds(0, total - rows), :], outb.at[a, j, pl.ds(0, total - rows), :], out_send.at[j, a]
            ).wait()
    for a in range(4):
        pltpu.make_async_copy(outs[a], outs[a], out_recv.at[a]).wait()


def put_out(*refs):
    sources, targets, sem = refs[:5], refs[5:11], refs[11]
    pairs = [*zip(sources[:4], targets[:4])]
    pairs += [(sources[4].at[i:i + 1], targets[4 + i]) for i in range(2)]
    copies = [pltpu.make_async_copy(a, b, sem.at[i]) for i, (a, b) in enumerate(pairs)]
    for copy in copies:
        copy.start()
    for copy in copies:
        copy.wait()


def shards(sizes, queries, keys, values, grad_out, q_gain, k_gain, clip_blocks):
    n, ny, nz = sizes
    rows, columns = queries.shape[1:]
    width = q_gain.shape[0]
    heads = columns // width // n
    total = rows * n
    hbm = pl.BlockSpec(memory_space=pltpu.HBM)
    landed = pl.BlockSpec(memory_space=pl.ANY)
    vmem = pl.BlockSpec(memory_space=pltpu.VMEM)
    wide = jax.ShapeDtypeStruct(queries.shape, jnp.bfloat16)
    half, full = jnp.bfloat16, jnp.float32
    result = pl.pallas_call(
        functools.partial(kernel, sizes, heads),
        name="attention_exchange",
        out_shape=(*(pltpu.VMEM(queries.shape, half) for _ in range(4)), pltpu.VMEM((8, width), full)),
        in_specs=[hbm] * 7,
        out_specs=(landed, landed, landed, landed, vmem),
        scratch_shapes=[
            pltpu.VMEM((1, width), full),
            pltpu.VMEM((1, width), full),
            pltpu.SMEM(clip_blocks.shape, jnp.int32),
            pltpu.SemaphoreType.DMA((3,)),
            pltpu.VMEM((4, heads, total, width), half),
            pltpu.VMEM((4, heads, total, width), half),
            pltpu.VMEM((total, width), half),
            pltpu.VMEM((width, total), half),
            pltpu.VMEM((total, width), half),
            pltpu.VMEM((width + 16, total), half),
            pltpu.VMEM((total, width), full),
            pltpu.VMEM((total, width), full),
            pltpu.VMEM((n, 8, width), full),
            pltpu.VMEM((ny, 8, width), full),
            pltpu.VMEM((nz, 8, width), full),
            pltpu.VMEM((8, width), full),
            pltpu.SemaphoreType.REGULAR,
            pltpu.SemaphoreType.DMA((heads, 4)),
            pltpu.SemaphoreType.DMA((heads, 4)),
            pltpu.SemaphoreType.DMA((heads, 4)),
            pltpu.SemaphoreType.DMA((4,)),
            pltpu.SemaphoreType.DMA((4, 8)),
            pltpu.SemaphoreType.DMA((4, 8)),
        ],
        compiler_params=pltpu.CompilerParams(
            collective_id=0, has_side_effects=True, vmem_limit_bytes=58 * 2**20
        ),
    )(queries, keys, values, grad_out, q_gain.reshape(1, width), k_gain.reshape(1, width), clip_blocks)
    gain = jax.ShapeDtypeStruct((1, width), full)
    *tensors, gain_q, gain_k = pl.pallas_call(
        put_out,
        name="put_out",
        out_shape=(wide, wide, wide, wide, gain, gain),
        in_specs=[landed] * 5,
        out_specs=[hbm] * 6,
        scratch_shapes=[pltpu.SemaphoreType.DMA((6,))],
        compiler_params=pltpu.CompilerParams(vmem_limit_bytes=8 * 2**20),
    )(*result)
    return *tensors, gain_q.reshape(width), gain_k.reshape(width)


def solution(mesh):
    n = mesh.shape["seq"]
    nz = 8
    ny = mesh.shape["dp"] // nz
    placed = P("dp", "seq", None)
    return jax.shard_map(
        functools.partial(shards, (n, ny, nz)),
        mesh=mesh,
        in_specs=(placed, placed, placed, placed, P(), P(), P()),
        out_specs=(placed, placed, placed, placed, P(), P()),
        check_vma=False,
    )
```

```python
import functools
import math

import jax
import jax.numpy as jnp
from jax import lax
from jax.experimental import pallas as pl
from jax.experimental.pallas import tpu as pltpu
from jax.sharding import PartitionSpec as P

BLOCK = 128
NORM_EPSILON = 1e-06
MESH = pl.DeviceIdType.MESH
QROWS = 512
HUB = 3
RELEASE = {
    "rest": (((0, 0), (0, 1)), ((0, 2), (0, 3), (1, 0), (1, 1), (1, 2), (1, 3))),
    "hub": (((0, 0), (0, 1), (0, 2)), ((0, 3), (1, 0)), ((1, 1), (1, 2), (1, 3))),
}
NT = (((1,), (1,)), ((), ()))
NN = (((1,), (0,)), ((), ()))


def dot(a, b, dims):
    return lax.dot_general(a, b, dims, preferred_element_type=jnp.float32)


def inverse_rms(x):
    return lax.rsqrt(jnp.mean(x * x, axis=-1, keepdims=True) + NORM_EPSILON)


def norm_back(x, r, gain, upstream):
    scaled = upstream * gain
    mean = jnp.mean(scaled * x, axis=-1, keepdims=True)
    grad = r * scaled - x * (r * r * r * mean)
    return grad, jnp.sum(upstream * x * r, axis=0, keepdims=True)


def kernel(sizes, heads, q_ref, k_ref, v_ref, g_ref, qg_hbm, kg_hbm, blocks_hbm,
           o_ref, dq_ref, dk_ref, dv_ref, gain_ref,
           qg_ref, kg_ref, blocks_ref, small_sem, inb, outb, keyc, keyt, valm, valt, q_norm, weight, out_inv, out_all, dk_acc, dv_acc, red_a, red_b, red_c, red_d, go_sem,
           in_send, in_recv, out_send, out_recv, red_send, red_recv):
    n, ny, nz = sizes
    dp = lax.axis_index("dp")
    me = lax.axis_index("seq")
    y, z = dp // nz, lax.rem(dp, nz)
    ins = (k_ref, v_ref, q_ref, g_ref)
    outs = (o_ref, dq_ref, dk_ref, dv_ref)
    rows = q_ref.shape[1]
    total = rows * n
    width = qg_ref.shape[1]

    smalls = [
        pltpu.make_async_copy(source, target, small_sem.at[i])
        for i, (source, target) in enumerate(
            ((qg_hbm, qg_ref), (kg_hbm, kg_ref), (blocks_hbm, blocks_ref))
        )
    ]
    for copy in smalls:
        copy.start()

    my_rows = pl.ds(pl.multiple_of(me * rows, rows), rows)

    def head_columns(device, j):
        return pl.ds(pl.multiple_of((device * heads + j) * width, width), width)

    for j in range(heads):
        for a in range(4):
            pltpu.make_async_copy(
                ins[a].at[0, :, head_columns(me, j)], inb.at[a, j, my_rows, :], in_recv.at[j, a]
            ).start()

    barrier = pltpu.get_barrier_semaphore()

    def greet(d, carry):
        peer = lax.rem(me + d, n)

        @pl.when(peer != HUB)
        def _():
            pl.semaphore_signal(barrier, inc=1, device_id=(dp, peer), device_id_type=MESH)

        return carry

    lax.fori_loop(1, n, greet, 0)

    @pl.when(me == HUB)
    def _():
        for d in range(1, ny):
            pl.semaphore_signal(barrier, inc=1, device_id=(lax.rem(y + d, ny) * nz + z, me), device_id_type=MESH)
        for d in range(1, nz):
            pl.semaphore_signal(barrier, inc=1, device_id=(y * nz + lax.rem(z + d, nz), me), device_id_type=MESH)

    @pl.when(me != HUB)
    def _():
        pl.semaphore_wait(barrier, n - 1)
        pl.semaphore_signal(go_sem, inc=1, device_id=(dp, HUB), device_id_type=MESH)

    @pl.when(me == HUB)
    def _():
        pl.semaphore_wait(go_sem, n - 1)

    for j in range(heads):
        for a in range(4):

            def send(d, carry, j=j, a=a):
                peer = lax.rem(me + d, n)
                pltpu.make_async_remote_copy(
                    src_ref=ins[a].at[0, :, head_columns(peer, j)],
                    dst_ref=inb.at[a, j, my_rows, :],
                    send_sem=in_send.at[j, a],
                    recv_sem=in_recv.at[j, a],
                    device_id=(dp, peer),
                    device_id_type=MESH,
                ).start()
                return carry

            lax.fori_loop(1, n, send, 0)

    for copy in smalls:
        copy.wait()
    length = blocks_ref[dp] * BLOCK
    q_gain = qg_ref[...]
    k_gain = kg_ref[...]
    scale = 1.0 / math.sqrt(width)
    key_scale = scale * math.log2(math.e)
    live_col = lax.broadcasted_iota(jnp.int32, (total, 1), 0) < length
    gain_q = jnp.zeros((1, width), jnp.float32)
    gain_k = jnp.zeros((1, width), jnp.float32)

    def give_back(j, arrays):
        def give(d, carry):
            peer = lax.rem(me + d, n)
            for a in arrays:
                pltpu.make_async_remote_copy(
                    src_ref=outb.at[a, j, pl.ds(pl.multiple_of(peer * rows, rows), rows), :],
                    dst_ref=outs[a].at[0, :, head_columns(me, j)],
                    send_sem=out_send.at[j, a],
                    recv_sem=out_recv.at[a],
                    device_id=(dp, peer),
                    device_id_type=MESH,
                ).start()
            return carry

        if len(arrays):
            lax.fori_loop(1, n, give, 0)

    def sent(a, j):
        piece = inb.at[a, j, pl.ds(0, total - rows), :]
        return pltpu.make_async_copy(piece, piece, in_send.at[j, a])

    def release(who, point):
        for j in range(heads):
            give_back(j, tuple(a for h, a in RELEASE[who][point] if h == j))

    def arrived(a, j):
        pltpu.make_async_copy(inb.at[a, j], inb.at[a, j], in_recv.at[j, a]).wait()

    for j in range(heads):
        arrived(0, j)
        k_float = inb[0, j].astype(jnp.float32)
        k_normed = jnp.where(live_col, k_float * inverse_rms(k_float) * (k_gain * key_scale), 0.0)
        keyc[...] = k_normed.astype(jnp.bfloat16)
        keyt[...] = k_normed.T.astype(jnp.bfloat16)
        arrived(1, j)
        v_float = jnp.where(live_col, inb[1, j].astype(jnp.float32), 0.0)
        valm[...] = v_float.astype(jnp.bfloat16)
        valt[0:width, :] = v_float.T.astype(jnp.bfloat16)
        live_lane = lax.broadcasted_iota(jnp.int32, (16, total), 1) < length
        valt[width:, :] = jnp.where(live_lane, 1.0, 0.0).astype(jnp.bfloat16)
        arrived(2, j)
        for at in range(0, total, QROWS):
            q_float = inb[2, j, at:at + QROWS, :].astype(jnp.float32)
            q_half = (q_float * inverse_rms(q_float) * q_gain).astype(jnp.bfloat16)
            q_norm[at:at + QROWS, :] = q_half
            e = jnp.exp2(dot(keyc[...], q_half, NT)).astype(jnp.bfloat16)
            weight[:, at:at + QROWS] = e
            out_ext = dot(valt[...], e, NN)
            live = at + lax.broadcasted_iota(jnp.int32, (1, QROWS), 1) < length
            inv = jnp.where(live, 1.0 / out_ext[width:width + 1, :], 0.0)
            out_t = out_ext[0:width, :] * inv
            out_inv[:, at:at + QROWS] = jnp.broadcast_to(inv, (8, QROWS))
            out_all[:, at:at + QROWS] = out_t
            outb[0, j, at:at + QROWS, :] = out_t.T.astype(jnp.bfloat16)

        arrived(3, j)
        for at in range(0, total, QROWS):
            e = weight[:, at:at + QROWS]
            q_half = q_norm[at:at + QROWS, :]
            g_t = inb[3, j, at:at + QROWS, :].astype(jnp.float32).T * out_inv[0:1, at:at + QROWS]
            gs = g_t.astype(jnp.bfloat16)
            row_dot = jnp.sum(g_t * out_all[:, at:at + QROWS], axis=0, keepdims=True)
            grad_probs = dot(valm[...], gs, NN)
            ds = (e.astype(jnp.float32) * (grad_probs - row_dot)).astype(jnp.bfloat16)
            add_v = dot(e, gs, NT)
            add_k = dot(ds, q_half, NN)
            if at == 0:
                dv_acc[...] = add_v
                dk_acc[...] = add_k
            else:
                dv_acc[...] += add_v
                dk_acc[...] += add_k
            grad_qnorm = dot(keyt[...], ds, NN).T * math.log(2.0)
            q_float = inb[2, j, at:at + QROWS, :].astype(jnp.float32)
            grad_q, part = norm_back(q_float, inverse_rms(q_float), q_gain, grad_qnorm)
            outb[1, j, at:at + QROWS, :] = grad_q.astype(jnp.bfloat16)
            gain_q = gain_q + part
        k_float = inb[0, j].astype(jnp.float32)
        grad_knorm = jnp.where(live_col, dk_acc[...] * scale, 0.0)
        grad_k, part = norm_back(k_float, inverse_rms(k_float), k_gain, grad_knorm)
        gain_k = gain_k + part
        outb[2, j] = grad_k.astype(jnp.bfloat16)
        outb[3, j] = jnp.where(live_col, dv_acc[...], 0.0).astype(jnp.bfloat16)

        for a in range(4):
            pltpu.make_async_copy(
                outb.at[a, j, my_rows, :], outs[a].at[0, :, head_columns(me, j)], out_recv.at[a]
            ).start()

        if j == 0:
            for a in range(4):
                sent(a, heads - 1).wait()

            @pl.when(me != HUB)
            def _():
                release("rest", 0)

            @pl.when(me == HUB)
            def _():
                release("hub", 0)

    def small(source, target, stage, slot, device):
        return pltpu.make_async_remote_copy(
            src_ref=source, dst_ref=target, send_sem=red_send.at[stage, slot], recv_sem=red_recv.at[stage, slot],
            device_id=device, device_id_type=MESH,
        )

    def gathered(slots):
        part = slots[0]
        for p in range(1, slots.shape[0]):
            part = part + slots[p]
        return part

    red_a[me] = jnp.concatenate([gain_q, gain_k, jnp.zeros((6, width), jnp.float32)], axis=0)

    @pl.when(me != HUB)
    def _():
        up = small(red_a.at[me], red_a.at[me], 0, me, (dp, HUB))
        up.start()
        release("rest", 1)
        up.wait_send()
        small(red_d, red_d, 3, me, (dp, HUB)).wait_recv()

    @pl.when(me == HUB)
    def _():
        for p in range(n):
            if p != HUB:
                small(red_a.at[p], red_a.at[p], 0, p, (dp, p)).wait_recv()
        red_b[y] = gathered(red_a)
        pl.semaphore_wait(barrier, ny + nz - 2)
        along_y = [
            small(red_b.at[y], red_b.at[y], 1, d, (lax.rem(y + d, ny) * nz + z, me)) for d in range(1, ny)
        ]
        for copy in along_y:
            copy.start()
        release("hub", 1)
        for copy in along_y:
            copy.wait()
        red_c[z] = gathered(red_b)
        along_z = [
            small(red_c.at[z], red_c.at[z], 2, d, (y * nz + lax.rem(z + d, nz), me)) for d in range(1, nz)
        ]
        for copy in along_z:
            copy.start()
        release("hub", 2)
        for copy in along_z:
            copy.wait()
        red_d[...] = gathered(red_c)
        down = [small(red_d, red_d, 3, p, (dp, p)) for p in range(n) if p != HUB]
        for copy in down:
            copy.start()
        for copy in down:
            copy.wait_send()

    gain_ref[...] = red_d[...]

    for j in range(heads):
        for a in range(4):
            if j < heads - 1:
                sent(a, j).wait()
            pltpu.make_async_copy(
                outb.at[a, j, pl.ds(0, total - rows), :], outb.at[a, j, pl.ds(0, total - rows), :], out_send.at[j, a]
            ).wait()
    for a in range(4):
        pltpu.make_async_copy(outs[a], outs[a], out_recv.at[a]).wait()


def put_out(*refs):
    sources, targets, sem = refs[:5], refs[5:11], refs[11]
    pairs = [*zip(sources[:4], targets[:4])]
    pairs += [(sources[4].at[i:i + 1], targets[4 + i]) for i in range(2)]
    copies = [pltpu.make_async_copy(a, b, sem.at[i]) for i, (a, b) in enumerate(pairs)]
    for copy in copies:
        copy.start()
    for copy in copies:
        copy.wait()


def shards(sizes, queries, keys, values, grad_out, q_gain, k_gain, clip_blocks):
    n, ny, nz = sizes
    rows, columns = queries.shape[1:]
    width = q_gain.shape[0]
    heads = columns // width // n
    total = rows * n
    hbm = pl.BlockSpec(memory_space=pltpu.HBM)
    landed = pl.BlockSpec(memory_space=pl.ANY)
    vmem = pl.BlockSpec(memory_space=pltpu.VMEM)
    wide = jax.ShapeDtypeStruct(queries.shape, jnp.bfloat16)
    half, full = jnp.bfloat16, jnp.float32
    result = pl.pallas_call(
        functools.partial(kernel, sizes, heads),
        name="attention_exchange",
        out_shape=(*(pltpu.VMEM(queries.shape, half) for _ in range(4)), pltpu.VMEM((8, width), full)),
        in_specs=[hbm] * 7,
        out_specs=(landed, landed, landed, landed, vmem),
        scratch_shapes=[
            pltpu.VMEM((1, width), full),
            pltpu.VMEM((1, width), full),
            pltpu.SMEM(clip_blocks.shape, jnp.int32),
            pltpu.SemaphoreType.DMA((3,)),
            pltpu.VMEM((4, heads, total, width), half),
            pltpu.VMEM((4, heads, total, width), half),
            pltpu.VMEM((total, width), half),
            pltpu.VMEM((width, total), half),
            pltpu.VMEM((total, width), half),
            pltpu.VMEM((width + 16, total), half),
            pltpu.VMEM((total, width), half),
            pltpu.VMEM((total, total), half),
            pltpu.VMEM((8, total), full),
            pltpu.VMEM((width, total), full),
            pltpu.VMEM((total, width), full),
            pltpu.VMEM((total, width), full),
            pltpu.VMEM((n, 8, width), full),
            pltpu.VMEM((ny, 8, width), full),
            pltpu.VMEM((nz, 8, width), full),
            pltpu.VMEM((8, width), full),
            pltpu.SemaphoreType.REGULAR,
            pltpu.SemaphoreType.DMA((heads, 4)),
            pltpu.SemaphoreType.DMA((heads, 4)),
            pltpu.SemaphoreType.DMA((heads, 4)),
            pltpu.SemaphoreType.DMA((4,)),
            pltpu.SemaphoreType.DMA((4, 8)),
            pltpu.SemaphoreType.DMA((4, 8)),
        ],
        compiler_params=pltpu.CompilerParams(
            collective_id=0, has_side_effects=True, vmem_limit_bytes=58 * 2**20
        ),
    )(queries, keys, values, grad_out, q_gain.reshape(1, width), k_gain.reshape(1, width), clip_blocks)
    gain = jax.ShapeDtypeStruct((1, width), full)
    *tensors, gain_q, gain_k = pl.pallas_call(
        put_out,
        name="put_out",
        out_shape=(wide, wide, wide, wide, gain, gain),
        in_specs=[landed] * 5,
        out_specs=[hbm] * 6,
        scratch_shapes=[pltpu.SemaphoreType.DMA((6,))],
        compiler_params=pltpu.CompilerParams(vmem_limit_bytes=8 * 2**20),
    )(*result)
    return *tensors, gain_q.reshape(width), gain_k.reshape(width)


def solution(mesh):
    n = mesh.shape["seq"]
    nz = 8
    ny = mesh.shape["dp"] // nz
    placed = P("dp", "seq", None)
    return jax.shard_map(
        functools.partial(shards, (n, ny, nz)),
        mesh=mesh,
        in_specs=(placed, placed, placed, placed, P(), P(), P()),
        out_specs=(placed, placed, placed, placed, P(), P()),
        check_vma=False,
    )
```

```python
import functools
import math

import jax
import jax.numpy as jnp
from jax import lax
from jax.experimental import pallas as pl
from jax.experimental.pallas import tpu as pltpu
from jax.sharding import PartitionSpec as P

BLOCK = 128
NORM_EPSILON = 1e-06
MESH = pl.DeviceIdType.MESH
QROWS = 512
HUB = 3
RELEASE = {
    "rest": (((0, 0), (0, 1)), ((0, 2), (0, 3), (1, 0), (1, 1), (1, 2), (1, 3))),
    "hub": (((0, 0), (0, 1), (0, 2)), ((0, 3), (1, 0)), ((1, 1), (1, 2), (1, 3))),
}
NT = (((1,), (1,)), ((), ()))
NN = (((1,), (0,)), ((), ()))


def dot(a, b, dims):
    return lax.dot_general(a, b, dims, preferred_element_type=jnp.float32)


def inverse_rms(x):
    return lax.rsqrt(jnp.mean(x * x, axis=-1, keepdims=True) + NORM_EPSILON)


def norm_back(x, r, gain, upstream):
    scaled = upstream * gain
    mean = jnp.mean(scaled * x, axis=-1, keepdims=True)
    grad = r * scaled - x * (r * r * r * mean)
    return grad, jnp.sum(upstream * x * r, axis=0, keepdims=True)


def kernel(sizes, heads, q_ref, k_ref, v_ref, g_ref, qg_hbm, kg_hbm, blocks_hbm,
           o_ref, dq_ref, dk_ref, dv_ref, gain_ref,
           qg_ref, kg_ref, blocks_ref, small_sem, inb, outb, keyc, keyt, valm, valt, q_norm, weight, out_inv, out_all, dk_acc, dv_acc, red_a, red_b, red_c, red_d, go_sem,
           in_send, in_recv, out_send, out_recv, red_send, red_recv):
    n, ny, nz = sizes
    dp = lax.axis_index("dp")
    me = lax.axis_index("seq")
    y, z = dp // nz, lax.rem(dp, nz)
    ins = (k_ref, v_ref, q_ref, g_ref)
    outs = (o_ref, dq_ref, dk_ref, dv_ref)
    rows = q_ref.shape[1]
    total = rows * n
    width = qg_ref.shape[1]

    barrier = pltpu.get_barrier_semaphore()

    def greet(d, carry):
        peer = lax.rem(me + d, n)

        @pl.when(peer != HUB)
        def _():
            pl.semaphore_signal(barrier, inc=1, device_id=(dp, peer), device_id_type=MESH)

        return carry

    lax.fori_loop(1, n, greet, 0)

    smalls = [
        pltpu.make_async_copy(source, target, small_sem.at[i])
        for i, (source, target) in enumerate(
            ((qg_hbm, qg_ref), (kg_hbm, kg_ref), (blocks_hbm, blocks_ref))
        )
    ]
    for copy in smalls:
        copy.start()

    my_rows = pl.ds(pl.multiple_of(me * rows, rows), rows)

    def head_columns(device, j):
        return pl.ds(pl.multiple_of((device * heads + j) * width, width), width)

    for j in range(heads):
        for a in range(4):
            pltpu.make_async_copy(
                ins[a].at[0, :, head_columns(me, j)], inb.at[a, j, my_rows, :], in_recv.at[j, a]
            ).start()

    @pl.when(me != HUB)
    def _():
        pl.semaphore_wait(barrier, n - 1)
        pl.semaphore_signal(go_sem, inc=1, device_id=(dp, HUB), device_id_type=MESH)

    @pl.when(me == HUB)
    def _():
        pl.semaphore_wait(go_sem, n - 1)

    for j in range(heads):
        for a in range(4):

            def send(d, carry, j=j, a=a):
                peer = lax.rem(me + d, n)
                pltpu.make_async_remote_copy(
                    src_ref=ins[a].at[0, :, head_columns(peer, j)],
                    dst_ref=inb.at[a, j, my_rows, :],
                    send_sem=in_send.at[j, a],
                    recv_sem=in_recv.at[j, a],
                    device_id=(dp, peer),
                    device_id_type=MESH,
                ).start()
                return carry

            lax.fori_loop(1, n, send, 0)

    @pl.when(me == HUB)
    def _():
        for d in range(1, ny):
            pl.semaphore_signal(barrier, inc=1, device_id=(lax.rem(y + d, ny) * nz + z, me), device_id_type=MESH)
        for d in range(1, nz):
            pl.semaphore_signal(barrier, inc=1, device_id=(y * nz + lax.rem(z + d, nz), me), device_id_type=MESH)

    for copy in smalls:
        copy.wait()
    length = blocks_ref[dp] * BLOCK
    q_gain = qg_ref[...]
    k_gain = kg_ref[...]
    scale = 1.0 / math.sqrt(width)
    key_scale = scale * math.log2(math.e)
    live_col = lax.broadcasted_iota(jnp.int32, (total, 1), 0) < length
    gain_q = jnp.zeros((1, width), jnp.float32)
    gain_k = jnp.zeros((1, width), jnp.float32)

    def give_back(j, arrays):
        def give(d, carry):
            peer = lax.rem(me + d, n)
            for a in arrays:
                pltpu.make_async_remote_copy(
                    src_ref=outb.at[a, j, pl.ds(pl.multiple_of(peer * rows, rows), rows), :],
                    dst_ref=outs[a].at[0, :, head_columns(me, j)],
                    send_sem=out_send.at[j, a],
                    recv_sem=out_recv.at[a],
                    device_id=(dp, peer),
                    device_id_type=MESH,
                ).start()
            return carry

        if len(arrays):
            lax.fori_loop(1, n, give, 0)

    def sent(a, j):
        piece = inb.at[a, j, pl.ds(0, total - rows), :]
        return pltpu.make_async_copy(piece, piece, in_send.at[j, a])

    def release(who, point):
        for j in range(heads):
            give_back(j, tuple(a for h, a in RELEASE[who][point] if h == j))

    def arrived(a, j):
        pltpu.make_async_copy(inb.at[a, j], inb.at[a, j], in_recv.at[j, a]).wait()

    for j in range(heads):
        arrived(0, j)
        k_float = inb[0, j].astype(jnp.float32)
        k_normed = jnp.where(live_col, k_float * inverse_rms(k_float) * (k_gain * key_scale), 0.0)
        keyc[...] = k_normed.astype(jnp.bfloat16)
        keyt[...] = k_normed.T.astype(jnp.bfloat16)
        arrived(1, j)
        v_float = jnp.where(live_col, inb[1, j].astype(jnp.float32), 0.0)
        valm[...] = v_float.astype(jnp.bfloat16)
        valt[0:width, :] = v_float.T.astype(jnp.bfloat16)
        live_lane = lax.broadcasted_iota(jnp.int32, (16, total), 1) < length
        valt[width:, :] = jnp.where(live_lane, 1.0, 0.0).astype(jnp.bfloat16)
        arrived(2, j)
        for at in range(0, total, QROWS):
            q_float = inb[2, j, at:at + QROWS, :].astype(jnp.float32)
            q_half = (q_float * inverse_rms(q_float) * q_gain).astype(jnp.bfloat16)
            q_norm[at:at + QROWS, :] = q_half
            e = jnp.exp2(dot(keyc[...], q_half, NT)).astype(jnp.bfloat16)
            weight[:, at:at + QROWS] = e
            out_ext = dot(valt[...], e, NN)
            live = at + lax.broadcasted_iota(jnp.int32, (1, QROWS), 1) < length
            inv = jnp.where(live, 1.0 / out_ext[width:width + 1, :], 0.0)
            out_t = out_ext[0:width, :] * inv
            out_inv[:, at:at + QROWS] = jnp.broadcast_to(inv, (8, QROWS))
            out_all[:, at:at + QROWS] = out_t
            outb[0, j, at:at + QROWS, :] = out_t.T.astype(jnp.bfloat16)

        arrived(3, j)
        for at in range(0, total, QROWS):
            e = weight[:, at:at + QROWS]
            q_half = q_norm[at:at + QROWS, :]
            g_t = inb[3, j, at:at + QROWS, :].astype(jnp.float32).T * out_inv[0:1, at:at + QROWS]
            gs = g_t.astype(jnp.bfloat16)
            row_dot = jnp.sum(g_t * out_all[:, at:at + QROWS], axis=0, keepdims=True)
            grad_probs = dot(valm[...], gs, NN)
            ds = (e.astype(jnp.float32) * (grad_probs - row_dot)).astype(jnp.bfloat16)
            add_v = dot(e, gs, NT)
            add_k = dot(ds, q_half, NN)
            if at == 0:
                dv_acc[...] = add_v
                dk_acc[...] = add_k
            else:
                dv_acc[...] += add_v
                dk_acc[...] += add_k
            grad_qnorm = dot(keyt[...], ds, NN).T * math.log(2.0)
            q_float = inb[2, j, at:at + QROWS, :].astype(jnp.float32)
            grad_q, part = norm_back(q_float, inverse_rms(q_float), q_gain, grad_qnorm)
            outb[1, j, at:at + QROWS, :] = grad_q.astype(jnp.bfloat16)
            gain_q = gain_q + part
        k_float = inb[0, j].astype(jnp.float32)
        grad_knorm = jnp.where(live_col, dk_acc[...] * scale, 0.0)
        grad_k, part = norm_back(k_float, inverse_rms(k_float), k_gain, grad_knorm)
        gain_k = gain_k + part
        outb[2, j] = grad_k.astype(jnp.bfloat16)
        outb[3, j] = jnp.where(live_col, dv_acc[...], 0.0).astype(jnp.bfloat16)

        for a in range(4):
            pltpu.make_async_copy(
                outb.at[a, j, my_rows, :], outs[a].at[0, :, head_columns(me, j)], out_recv.at[a]
            ).start()

        if j == 0:
            for a in range(4):
                sent(a, heads - 1).wait()

            @pl.when(me != HUB)
            def _():
                release("rest", 0)

            @pl.when(me == HUB)
            def _():
                release("hub", 0)

    def small(source, target, stage, slot, device):
        return pltpu.make_async_remote_copy(
            src_ref=source, dst_ref=target, send_sem=red_send.at[stage, slot], recv_sem=red_recv.at[stage, slot],
            device_id=device, device_id_type=MESH,
        )

    def gathered(slots):
        part = slots[0]
        for p in range(1, slots.shape[0]):
            part = part + slots[p]
        return part

    red_a[me] = jnp.concatenate([gain_q, gain_k, jnp.zeros((6, width), jnp.float32)], axis=0)

    @pl.when(me != HUB)
    def _():
        up = small(red_a.at[me], red_a.at[me], 0, me, (dp, HUB))
        up.start()
        release("rest", 1)
        up.wait_send()
        small(red_d, red_d, 3, me, (dp, HUB)).wait_recv()

    @pl.when(me == HUB)
    def _():
        for p in range(n):
            if p != HUB:
                small(red_a.at[p], red_a.at[p], 0, p, (dp, p)).wait_recv()
        red_b[y] = gathered(red_a)
        pl.semaphore_wait(barrier, ny + nz - 2)
        along_y = [
            small(red_b.at[y], red_b.at[y], 1, d, (lax.rem(y + d, ny) * nz + z, me)) for d in range(1, ny)
        ]
        for copy in along_y:
            copy.start()
        release("hub", 1)
        for copy in along_y:
            copy.wait()
        red_c[z] = gathered(red_b)
        along_z = [
            small(red_c.at[z], red_c.at[z], 2, d, (y * nz + lax.rem(z + d, nz), me)) for d in range(1, nz)
        ]
        for copy in along_z:
            copy.start()
        release("hub", 2)
        for copy in along_z:
            copy.wait()
        red_d[...] = gathered(red_c)
        down = [small(red_d, red_d, 3, p, (dp, p)) for p in range(n) if p != HUB]
        for copy in down:
            copy.start()
        for copy in down:
            copy.wait_send()

    gain_ref[...] = red_d[...]

    for j in range(heads):
        for a in range(4):
            if j < heads - 1:
                sent(a, j).wait()
            pltpu.make_async_copy(
                outb.at[a, j, pl.ds(0, total - rows), :], outb.at[a, j, pl.ds(0, total - rows), :], out_send.at[j, a]
            ).wait()
    for a in range(4):
        pltpu.make_async_copy(outs[a], outs[a], out_recv.at[a]).wait()


def put_out(*refs):
    sources, targets, sem = refs[:5], refs[5:11], refs[11]
    pairs = [*zip(sources[:4], targets[:4])]
    pairs += [(sources[4].at[i:i + 1], targets[4 + i]) for i in range(2)]
    copies = [pltpu.make_async_copy(a, b, sem.at[i]) for i, (a, b) in enumerate(pairs)]
    for copy in copies:
        copy.start()
    for copy in copies:
        copy.wait()


def shards(sizes, queries, keys, values, grad_out, q_gain, k_gain, clip_blocks):
    n, ny, nz = sizes
    rows, columns = queries.shape[1:]
    width = q_gain.shape[0]
    heads = columns // width // n
    total = rows * n
    hbm = pl.BlockSpec(memory_space=pltpu.HBM)
    landed = pl.BlockSpec(memory_space=pl.ANY)
    vmem = pl.BlockSpec(memory_space=pltpu.VMEM)
    wide = jax.ShapeDtypeStruct(queries.shape, jnp.bfloat16)
    half, full = jnp.bfloat16, jnp.float32
    result = pl.pallas_call(
        functools.partial(kernel, sizes, heads),
        name="attention_exchange",
        out_shape=(*(pltpu.VMEM(queries.shape, half) for _ in range(4)), pltpu.VMEM((8, width), full)),
        in_specs=[hbm] * 7,
        out_specs=(landed, landed, landed, landed, vmem),
        scratch_shapes=[
            pltpu.VMEM((1, width), full),
            pltpu.VMEM((1, width), full),
            pltpu.SMEM(clip_blocks.shape, jnp.int32),
            pltpu.SemaphoreType.DMA((3,)),
            pltpu.VMEM((4, heads, total, width), half),
            pltpu.VMEM((4, heads, total, width), half),
            pltpu.VMEM((total, width), half),
            pltpu.VMEM((width, total), half),
            pltpu.VMEM((total, width), half),
            pltpu.VMEM((width + 16, total), half),
            pltpu.VMEM((total, width), half),
            pltpu.VMEM((total, total), half),
            pltpu.VMEM((8, total), full),
            pltpu.VMEM((width, total), full),
            pltpu.VMEM((total, width), full),
            pltpu.VMEM((total, width), full),
            pltpu.VMEM((n, 8, width), full),
            pltpu.VMEM((ny, 8, width), full),
            pltpu.VMEM((nz, 8, width), full),
            pltpu.VMEM((8, width), full),
            pltpu.SemaphoreType.REGULAR,
            pltpu.SemaphoreType.DMA((heads, 4)),
            pltpu.SemaphoreType.DMA((heads, 4)),
            pltpu.SemaphoreType.DMA((heads, 4)),
            pltpu.SemaphoreType.DMA((4,)),
            pltpu.SemaphoreType.DMA((4, 8)),
            pltpu.SemaphoreType.DMA((4, 8)),
        ],
        compiler_params=pltpu.CompilerParams(
            collective_id=0, has_side_effects=True, vmem_limit_bytes=58 * 2**20
        ),
    )(queries, keys, values, grad_out, q_gain.reshape(1, width), k_gain.reshape(1, width), clip_blocks)
    gain = jax.ShapeDtypeStruct((1, width), full)
    *tensors, gain_q, gain_k = pl.pallas_call(
        put_out,
        name="put_out",
        out_shape=(wide, wide, wide, wide, gain, gain),
        in_specs=[landed] * 5,
        out_specs=[hbm] * 6,
        scratch_shapes=[pltpu.SemaphoreType.DMA((6,))],
        compiler_params=pltpu.CompilerParams(vmem_limit_bytes=8 * 2**20),
    )(*result)
    return *tensors, gain_q.reshape(width), gain_k.reshape(width)


def solution(mesh):
    n = mesh.shape["seq"]
    nz = 8
    ny = mesh.shape["dp"] // nz
    placed = P("dp", "seq", None)
    return jax.shard_map(
        functools.partial(shards, (n, ny, nz)),
        mesh=mesh,
        in_specs=(placed, placed, placed, placed, P(), P(), P()),
        out_specs=(placed, placed, placed, placed, P(), P()),
        check_vma=False,
    )
```

```python
import functools
import math

import jax
import jax.numpy as jnp
from jax import lax
from jax.experimental import pallas as pl
from jax.experimental.pallas import tpu as pltpu
from jax.sharding import PartitionSpec as P

BLOCK = 128
NORM_EPSILON = 1e-06
MESH = pl.DeviceIdType.MESH
QROWS = 512
HUB = 3
RELEASE = {
    "rest": (((0, 0), (0, 1)), ((0, 2), (0, 3), (1, 0), (1, 1), (1, 2), (1, 3))),
    "hub": (((0, 0), (0, 1), (0, 2)), ((0, 3), (1, 0)), ((1, 1), (1, 2), (1, 3))),
}
NT = (((1,), (1,)), ((), ()))
NN = (((1,), (0,)), ((), ()))


def dot(a, b, dims):
    return lax.dot_general(a, b, dims, preferred_element_type=jnp.float32)


def inverse_rms(x):
    return lax.rsqrt(jnp.mean(x * x, axis=-1, keepdims=True) + NORM_EPSILON)


def norm_back(x, r, gain, upstream):
    scaled = upstream * gain
    mean = jnp.mean(scaled * x, axis=-1, keepdims=True)
    grad = r * scaled - x * (r * r * r * mean)
    return grad, jnp.sum(upstream * x * r, axis=0, keepdims=True)


def kernel(sizes, heads, q_ref, k_ref, v_ref, g_ref, qg_hbm, kg_hbm, blocks_hbm,
           o_ref, dq_ref, dk_ref, dv_ref, gain_ref,
           qg_ref, kg_ref, blocks_ref, small_sem, inb, outb, keyc, keyt, valm, valt, q_norm, weight, out_inv, out_all, dk_acc, dv_acc, red_a, red_b, red_c, red_d, go_sem,
           in_send, in_recv, out_send, out_recv, red_send, red_recv):
    n, ny, nz = sizes
    dp = lax.axis_index("dp")
    me = lax.axis_index("seq")
    y, z = dp // nz, lax.rem(dp, nz)
    ins = (k_ref, v_ref, q_ref, g_ref)
    outs = (o_ref, dq_ref, dk_ref, dv_ref)
    rows = q_ref.shape[1]
    total = rows * n
    width = qg_ref.shape[1]

    barrier = pltpu.get_barrier_semaphore()

    def greet(d, carry):
        peer = lax.rem(me + d, n)

        @pl.when(peer != HUB)
        def _():
            pl.semaphore_signal(barrier, inc=1, device_id=(dp, peer), device_id_type=MESH)

        return carry

    lax.fori_loop(1, n, greet, 0)

    smalls = [
        pltpu.make_async_copy(source, target, small_sem.at[i])
        for i, (source, target) in enumerate(
            ((qg_hbm, qg_ref), (kg_hbm, kg_ref), (blocks_hbm, blocks_ref))
        )
    ]
    for copy in smalls:
        copy.start()

    my_rows = pl.ds(pl.multiple_of(me * rows, rows), rows)

    def head_columns(device, j):
        return pl.ds(pl.multiple_of((device * heads + j) * width, width), width)

    for j in range(heads):
        for a in range(4):
            pltpu.make_async_copy(
                ins[a].at[0, :, head_columns(me, j)], inb.at[a, j, my_rows, :], in_recv.at[j, a]
            ).start()

    @pl.when(me != HUB)
    def _():
        pl.semaphore_wait(barrier, n - 1)
        pl.semaphore_signal(go_sem, inc=1, device_id=(dp, HUB), device_id_type=MESH)

    @pl.when(me == HUB)
    def _():
        pl.semaphore_wait(go_sem, n - 1)

    for j in range(heads):
        for a in range(4):

            def send(d, carry, j=j, a=a):
                peer = lax.rem(me + d, n)
                pltpu.make_async_remote_copy(
                    src_ref=ins[a].at[0, :, head_columns(peer, j)],
                    dst_ref=inb.at[a, j, my_rows, :],
                    send_sem=in_send.at[j, a],
                    recv_sem=in_recv.at[j, a],
                    device_id=(dp, peer),
                    device_id_type=MESH,
                ).start()
                return carry

            lax.fori_loop(1, n, send, 0)

    @pl.when(me == HUB)
    def _():
        for d in range(1, ny):
            pl.semaphore_signal(barrier, inc=1, device_id=(lax.rem(y + d, ny) * nz + z, me), device_id_type=MESH)
        for d in range(1, nz):
            pl.semaphore_signal(barrier, inc=1, device_id=(y * nz + lax.rem(z + d, nz), me), device_id_type=MESH)

    for copy in smalls:
        copy.wait()
    length = blocks_ref[dp] * BLOCK
    q_gain = qg_ref[...]
    k_gain = kg_ref[...]
    scale = 1.0 / math.sqrt(width)
    key_scale = scale * math.log2(math.e)
    live_col = lax.broadcasted_iota(jnp.int32, (total, 1), 0) < length
    gain_q = jnp.zeros((1, width), jnp.float32)
    gain_k = jnp.zeros((1, width), jnp.float32)

    def give_back(j, arrays):
        def give(d, carry):
            peer = lax.rem(me + d, n)
            for a in arrays:
                pltpu.make_async_remote_copy(
                    src_ref=outb.at[a, j, pl.ds(pl.multiple_of(peer * rows, rows), rows), :],
                    dst_ref=outs[a].at[0, :, head_columns(me, j)],
                    send_sem=out_send.at[j, a],
                    recv_sem=out_recv.at[a],
                    device_id=(dp, peer),
                    device_id_type=MESH,
                ).start()
            return carry

        if len(arrays):
            lax.fori_loop(1, n, give, 0)

    def sent(a, j):
        piece = inb.at[a, j, pl.ds(0, total - rows), :]
        return pltpu.make_async_copy(piece, piece, in_send.at[j, a])

    def release(who, point):
        for j in range(heads):
            give_back(j, tuple(a for h, a in RELEASE[who][point] if h == j))

    def arrived(a, j):
        pltpu.make_async_copy(inb.at[a, j], inb.at[a, j], in_recv.at[j, a]).wait()

    for j in range(heads):
        arrived(0, j)
        k_float = inb[0, j].astype(jnp.float32)
        k_normed = jnp.where(live_col, k_float * inverse_rms(k_float) * (k_gain * key_scale), 0.0)
        keyc[...] = k_normed.astype(jnp.bfloat16)
        keyt[...] = keyc[...].T
        arrived(1, j)
        valm[...] = jnp.where(live_col, inb[1, j].astype(jnp.float32), 0.0).astype(jnp.bfloat16)
        valt[0:width, :] = valm[...].T
        live_lane = lax.broadcasted_iota(jnp.int32, (16, total), 1) < length
        valt[width:, :] = jnp.where(live_lane, 1.0, 0.0).astype(jnp.bfloat16)
        arrived(2, j)
        for at in range(0, total, QROWS):
            q_float = inb[2, j, at:at + QROWS, :].astype(jnp.float32)
            q_half = (q_float * inverse_rms(q_float) * q_gain).astype(jnp.bfloat16)
            q_norm[at:at + QROWS, :] = q_half
            e = jnp.exp2(dot(keyc[...], q_half, NT)).astype(jnp.bfloat16)
            weight[:, at:at + QROWS] = e
            out_ext = dot(valt[...], e, NN)
            live = at + lax.broadcasted_iota(jnp.int32, (1, QROWS), 1) < length
            inv = jnp.where(live, 1.0 / out_ext[width:width + 1, :], 0.0)
            out_t = out_ext[0:width, :] * inv
            out_inv[:, at:at + QROWS] = jnp.broadcast_to(inv, (8, QROWS))
            out_all[:, at:at + QROWS] = out_t
            outb[0, j, at:at + QROWS, :] = out_t.T.astype(jnp.bfloat16)

        arrived(3, j)
        for at in range(0, total, QROWS):
            e = weight[:, at:at + QROWS]
            q_half = q_norm[at:at + QROWS, :]
            g_t = inb[3, j, at:at + QROWS, :].T.astype(jnp.float32) * out_inv[0:1, at:at + QROWS]
            gs = g_t.astype(jnp.bfloat16)
            row_dot = jnp.sum(g_t * out_all[:, at:at + QROWS], axis=0, keepdims=True)
            grad_probs = dot(valm[...], gs, NN)
            ds = (e.astype(jnp.float32) * (grad_probs - row_dot)).astype(jnp.bfloat16)
            add_v = dot(e, gs, NT)
            add_k = dot(ds, q_half, NN)
            if at == 0:
                dv_acc[...] = add_v
                dk_acc[...] = add_k
            else:
                dv_acc[...] += add_v
                dk_acc[...] += add_k
            grad_qnorm = dot(keyt[...], ds, NN).T * math.log(2.0)
            q_float = inb[2, j, at:at + QROWS, :].astype(jnp.float32)
            grad_q, part = norm_back(q_float, inverse_rms(q_float), q_gain, grad_qnorm)
            outb[1, j, at:at + QROWS, :] = grad_q.astype(jnp.bfloat16)
            gain_q = gain_q + part
        k_float = inb[0, j].astype(jnp.float32)
        grad_knorm = jnp.where(live_col, dk_acc[...] * scale, 0.0)
        grad_k, part = norm_back(k_float, inverse_rms(k_float), k_gain, grad_knorm)
        gain_k = gain_k + part
        outb[2, j] = grad_k.astype(jnp.bfloat16)
        outb[3, j] = jnp.where(live_col, dv_acc[...], 0.0).astype(jnp.bfloat16)

        for a in range(4):
            pltpu.make_async_copy(
                outb.at[a, j, my_rows, :], outs[a].at[0, :, head_columns(me, j)], out_recv.at[a]
            ).start()

        if j == 0:
            for a in range(4):
                sent(a, heads - 1).wait()

            @pl.when(me != HUB)
            def _():
                release("rest", 0)

            @pl.when(me == HUB)
            def _():
                release("hub", 0)

    def small(source, target, stage, slot, device):
        return pltpu.make_async_remote_copy(
            src_ref=source, dst_ref=target, send_sem=red_send.at[stage, slot], recv_sem=red_recv.at[stage, slot],
            device_id=device, device_id_type=MESH,
        )

    def gathered(slots):
        part = slots[0]
        for p in range(1, slots.shape[0]):
            part = part + slots[p]
        return part

    red_a[me] = jnp.concatenate([gain_q, gain_k, jnp.zeros((6, width), jnp.float32)], axis=0)

    @pl.when(me != HUB)
    def _():
        up = small(red_a.at[me], red_a.at[me], 0, me, (dp, HUB))
        up.start()
        release("rest", 1)
        up.wait_send()
        small(red_d, red_d, 3, me, (dp, HUB)).wait_recv()

    @pl.when(me == HUB)
    def _():
        for p in range(n):
            if p != HUB:
                small(red_a.at[p], red_a.at[p], 0, p, (dp, p)).wait_recv()
        red_b[y] = gathered(red_a)
        pl.semaphore_wait(barrier, ny + nz - 2)
        along_y = [
            small(red_b.at[y], red_b.at[y], 1, d, (lax.rem(y + d, ny) * nz + z, me)) for d in range(1, ny)
        ]
        for copy in along_y:
            copy.start()
        release("hub", 1)
        for copy in along_y:
            copy.wait()
        red_c[z] = gathered(red_b)
        along_z = [
            small(red_c.at[z], red_c.at[z], 2, d, (y * nz + lax.rem(z + d, nz), me)) for d in range(1, nz)
        ]
        for copy in along_z:
            copy.start()
        release("hub", 2)
        for copy in along_z:
            copy.wait()
        red_d[...] = gathered(red_c)
        down = [small(red_d, red_d, 3, p, (dp, p)) for p in range(n) if p != HUB]
        for copy in down:
            copy.start()
        for copy in down:
            copy.wait_send()

    gain_ref[...] = red_d[...]

    for j in range(heads):
        for a in range(4):
            if j < heads - 1:
                sent(a, j).wait()
            pltpu.make_async_copy(
                outb.at[a, j, pl.ds(0, total - rows), :], outb.at[a, j, pl.ds(0, total - rows), :], out_send.at[j, a]
            ).wait()
    for a in range(4):
        pltpu.make_async_copy(outs[a], outs[a], out_recv.at[a]).wait()


def put_out(*refs):
    sources, targets, sem = refs[:5], refs[5:11], refs[11]
    pairs = [*zip(sources[:4], targets[:4])]
    pairs += [(sources[4].at[i:i + 1], targets[4 + i]) for i in range(2)]
    copies = [pltpu.make_async_copy(a, b, sem.at[i]) for i, (a, b) in enumerate(pairs)]
    for copy in copies:
        copy.start()
    for copy in copies:
        copy.wait()


def shards(sizes, queries, keys, values, grad_out, q_gain, k_gain, clip_blocks):
    n, ny, nz = sizes
    rows, columns = queries.shape[1:]
    width = q_gain.shape[0]
    heads = columns // width // n
    total = rows * n
    hbm = pl.BlockSpec(memory_space=pltpu.HBM)
    landed = pl.BlockSpec(memory_space=pl.ANY)
    vmem = pl.BlockSpec(memory_space=pltpu.VMEM)
    wide = jax.ShapeDtypeStruct(queries.shape, jnp.bfloat16)
    half, full = jnp.bfloat16, jnp.float32
    result = pl.pallas_call(
        functools.partial(kernel, sizes, heads),
        name="attention_exchange",
        out_shape=(*(pltpu.VMEM(queries.shape, half) for _ in range(4)), pltpu.VMEM((8, width), full)),
        in_specs=[hbm] * 7,
        out_specs=(landed, landed, landed, landed, vmem),
        scratch_shapes=[
            pltpu.VMEM((1, width), full),
            pltpu.VMEM((1, width), full),
            pltpu.SMEM(clip_blocks.shape, jnp.int32),
            pltpu.SemaphoreType.DMA((3,)),
            pltpu.VMEM((4, heads, total, width), half),
            pltpu.VMEM((4, heads, total, width), half),
            pltpu.VMEM((total, width), half),
            pltpu.VMEM((width, total), half),
            pltpu.VMEM((total, width), half),
            pltpu.VMEM((width + 16, total), half),
            pltpu.VMEM((total, width), half),
            pltpu.VMEM((total, total), half),
            pltpu.VMEM((8, total), full),
            pltpu.VMEM((width, total), full),
            pltpu.VMEM((total, width), full),
            pltpu.VMEM((total, width), full),
            pltpu.VMEM((n, 8, width), full),
            pltpu.VMEM((ny, 8, width), full),
            pltpu.VMEM((nz, 8, width), full),
            pltpu.VMEM((8, width), full),
            pltpu.SemaphoreType.REGULAR,
            pltpu.SemaphoreType.DMA((heads, 4)),
            pltpu.SemaphoreType.DMA((heads, 4)),
            pltpu.SemaphoreType.DMA((heads, 4)),
            pltpu.SemaphoreType.DMA((4,)),
            pltpu.SemaphoreType.DMA((4, 8)),
            pltpu.SemaphoreType.DMA((4, 8)),
        ],
        compiler_params=pltpu.CompilerParams(
            collective_id=0, has_side_effects=True, vmem_limit_bytes=58 * 2**20
        ),
    )(queries, keys, values, grad_out, q_gain.reshape(1, width), k_gain.reshape(1, width), clip_blocks)
    gain = jax.ShapeDtypeStruct((1, width), full)
    *tensors, gain_q, gain_k = pl.pallas_call(
        put_out,
        name="put_out",
        out_shape=(wide, wide, wide, wide, gain, gain),
        in_specs=[landed] * 5,
        out_specs=[hbm] * 6,
        scratch_shapes=[pltpu.SemaphoreType.DMA((6,))],
        compiler_params=pltpu.CompilerParams(vmem_limit_bytes=8 * 2**20),
    )(*result)
    return *tensors, gain_q.reshape(width), gain_k.reshape(width)


def solution(mesh):
    n = mesh.shape["seq"]
    nz = 8
    ny = mesh.shape["dp"] // nz
    placed = P("dp", "seq", None)
    return jax.shard_map(
        functools.partial(shards, (n, ny, nz)),
        mesh=mesh,
        in_specs=(placed, placed, placed, placed, P(), P(), P()),
        out_specs=(placed, placed, placed, placed, P(), P()),
        check_vma=False,
    )
```
